128 devices in a mesh: island: 4 (over y_hi, core), fsdp: 32 (over z, y_lo, x).
Axes of the slice: x: 4, y: 4 (y_hi: 2, y_lo: 2; y = y_hi * 2 + y_lo), z: 4, core: 2. Of those that a mesh axis runs over, the one named last changes fastest.
Arguments:
- hidden: bfloat16 [4, 24576, 7168], P('island', 'fsdp'), may hold values from -6 to 6
- grad_out: bfloat16 [4, 24576, 2048], P('island', 'fsdp'), may hold values from -0.076171875 to 0.076171875
- inner_params: float32 [4, 7168, 2048], P('island', 'fsdp'), may hold values from -6 to 6
- first_moment: float32 [4, 7168, 2048], P('island', 'fsdp'), may hold values from -6 to 6
- second_moment: float32 [4, 7168, 2048], P('island', 'fsdp'), may hold values from 0.25 to 16
- anchor: float32 [7168, 2048], P('fsdp', 'island'), may hold values from -6 to 6
- outer_momentum: float32 [7168, 2048], P('fsdp', 'island'), may hold values from -3 to 3
Outputs:
- new_params: bfloat16 [7168, 2048], P('fsdp')
- new_momentum: float32 [7168, 2048], P('fsdp', 'island')
- new_first: float32 [4, 7168, 2048], P('island', 'fsdp')
- new_second: float32 [4, 7168, 2048], P('island', 'fsdp')
The draws below stay inside these ranges and needn't reach their ends.
All inputs are finite; a program needn't handle non-finite values.
Results may differ from the reference program's by a relative error of at most 0.015.
Values may be sent and summed in bfloat16 or wider, within the bound.
A program may use at most 128 MiB of HBM per device.

```python
import math
import jax
import jax.numpy as jnp
from jax import lax

D = 2048
FF = 7168
TOK_DEV = 768
INNER_STEP = 20
TOKENS = 24576
ISLANDS = 4
N_FSDP = 32


def strengthened(values, rng, source, target, shards_of, factor):
    def block_of(axis_at):
        return (jnp.arange(values.shape[axis_at]) // (values.shape[axis_at] // shards_of)).reshape((-1,) + (1,) * (values.ndim - 1 - axis_at))

    first = jax.random.permutation(rng, shards_of)[block_of(target)]
    other_side = (block_of(target) + shards_of // 2) % shards_of
    return jnp.where((block_of(source) == first) | (block_of(source) == other_side), factor * values, values)


def level_of(rng, dims, split, smallest, high):
    gain, own = 1.0, jax.random.fold_in(rng, 6)
    for axis_at, parts in split:
        steps = jnp.exp(jax.random.uniform(jax.random.fold_in(own, axis_at), (parts,), jnp.float32, smallest / len(split), high / len(split)))
        gain = gain * jnp.repeat(steps, dims[axis_at] // parts).reshape([-1 if axis == axis_at else 1 for axis in range(len(dims))])
    return gain


def scatter_about(key, shape, deviation, most, pieces=(), held_as=jnp.bfloat16):
    gain = level_of(key, shape, pieces, -0.22, 0.18) if pieces else 1.0
    drawn = jax.random.normal(key, shape, jnp.float32) * deviation * gain
    return jnp.minimum(jnp.maximum(drawn, -most), most).astype(held_as)


def bell_draw_with(rng, dims, spread, most, split, heavy, held_as=jnp.bfloat16):
    array = spread * jax.random.normal(rng, dims, jnp.float32)
    if split:
        array = array * level_of(rng, dims, split, -0.22, 0.18)
    return jnp.clip(strengthened(array, jax.random.fold_in(rng, 3), *heavy), -most, most).astype(held_as)


def setup_inputs(seed: int = 0) -> dict:
    keys = jax.random.split(jax.random.key(seed), 8)
    hidden = bell_draw_with(keys[0], (ISLANDS, TOKENS, FF), 1.0, 6.0, ((0, 4), (1, 32)), (1, 2, 32, 2.75))
    grad_out = scatter_about(keys[1], (ISLANDS, TOKENS, D), (2.0 / (TOK_DEV * N_FSDP) ** 0.5), 0.076171875, ((0, 4), (1, 32)))
    inner_params = scatter_about(keys[2], (ISLANDS, FF, D), 1.0, 6.0, ((0, 4), (1, 32)), jnp.float32)
    first_moment = scatter_about(keys[3], (ISLANDS, FF, D), 1.0, 6.0, ((0, 4), (1, 32)), jnp.float32)
    second_moment = jnp.clip(jnp.exp(math.log(16.0) - 4.158883 * jax.random.uniform(keys[4], (ISLANDS, FF, D), jnp.float32) ** level_of(keys[4], (ISLANDS, FF, D), ((0, 4), (1, 32)), -0.2, 0.2)), 0.25, 16.0)
    anchor = scatter_about(keys[5], (FF, D), 1.0, 6.0, ((0, 32), (1, 4)), jnp.float32)
    outer_momentum = scatter_about(keys[6], (FF, D), 0.5, 3.0, ((0, 32), (1, 4)), jnp.float32)
    return dict(hidden=hidden, grad_out=grad_out, inner_params=inner_params, first_moment=first_moment, second_moment=second_moment, anchor=anchor, outer_momentum=outer_momentum)


beta_one = 0.9
beta_two = 0.95
inner_rate = 0.01
decay_rate = 0.1
adam_eps = 1e-08
outer_rate = 0.7
outer_beta = 0.9

def island_gradient(hidden_island, grad_island):
    blocks_h = hidden_island.reshape(N_FSDP, TOK_DEV, FF)
    blocks_g = grad_island.reshape(N_FSDP, TOK_DEV, D)

    def accumulate(total, pair):
        part = lax.dot_general(pair[0], pair[1], (((0,), (0,)), ((), ())), preferred_element_type=jnp.float32)
        part = lax.optimization_barrier(part.astype(jnp.bfloat16)).astype(jnp.float32)
        return (total + part, None)
    total, unused = lax.scan(accumulate, jnp.zeros((FF, D), jnp.float32), (blocks_h, blocks_g))
    return total

def reference(hidden, grad_out, inner_params, first_moment, second_moment, anchor, outer_momentum):
    corr_one = 1.0 - beta_one ** INNER_STEP
    corr_two = 1.0 - beta_two ** INNER_STEP
    firsts = []
    seconds = []
    summed = jnp.zeros((FF, D), jnp.float32)
    for island in range(ISLANDS):
        gradient = island_gradient(hidden[island], grad_out[island])
        first = beta_one * first_moment[island] + (1.0 - beta_one) * gradient
        second = beta_two * second_moment[island] + (1.0 - beta_two) * gradient * gradient
        update = first / corr_one / (jnp.sqrt(second / corr_two) + adam_eps)
        stepped = inner_params[island] - inner_rate * (update + decay_rate * inner_params[island])
        summed = summed + stepped
        firsts.append(first)
        seconds.append(second)
    pseudo = anchor - summed / ISLANDS
    new_momentum = outer_beta * outer_momentum + pseudo
    new_params = (anchor - outer_rate * (pseudo + outer_beta * new_momentum)).astype(jnp.bfloat16)
    return (new_params, new_momentum, jnp.stack(firsts), jnp.stack(seconds))
```

```python
import functools

import jax
import jax.numpy as jnp
from jax import lax
from jax.experimental import pallas as pl
from jax.experimental.pallas import tpu as pltpu
from jax.sharding import PartitionSpec as P

INNER_STEP = 20
beta_one = 0.9
beta_two = 0.95
inner_rate = 0.01
decay_rate = 0.1
adam_eps = 1e-08
outer_rate = 0.7
outer_beta = 0.9

MESH = pl.DeviceIdType.MESH
TOK, FF, D = 768, 7168, 2048
ROWS, HALF = 224, 112
QROWS = 4 * ROWS
WIDE = 256
GROUPS = 4
STEPS = 8 * GROUPS
SLOTS = 16
D1, D2, D3, D4, D5 = 2, 4, 6, 8, 11
F32, BF16 = jnp.float32, jnp.bfloat16


ROWS_Y = 32
LATE = ROWS - ROWS_Y


def offset_of(q):
    return jnp.where(q == 2, 3, jnp.where(q == 3, 0, 2 - q))


def kernel(
    hid, gra, par_h, mom_h, var_h, anc_h, out_h,
    o_par, o_mom, o_first, o_second,
    hch, hT, G, par, mom, var, anc, om,
    ring, ey, sy, c1, tb, tf, st, nbuf,
    rA, rYE, rY, rC, rE,
    ld, hs, sA, sYE, sY, sC, sE, sN, outs, loc,
    qA, qYE, qY, qC, qE, qN,
):
    isl, f = lax.axis_index("island"), lax.axis_index("fsdp")
    yh, co = isl // 2, isl % 2
    z, y, x = f // 8, (f // 4) % 2, f % 4
    other_y = 1 - y

    def fs(zz, yy, xx):
        return zz * 8 + yy * 4 + xx

    xr, xl = (isl, fs(z, y, (x + 1) % 4)), (isl, fs(z, y, (x + 3) % 4))
    zr, zl = (isl, fs((z + 1) % 4, y, x)), (isl, fs((z + 3) % 4, y, x))
    ynb = (isl, fs(z, other_y, x))
    A = ((xr, xl), (zr, zl))
    C = ((zr, zl), (xr, xl))
    a_of = (x, z)
    c_of = (z, x)

    def block(k, a, yy, c):
        return fs(c, yy, a) if k == 0 else fs(a, yy, c)

    def chunk_q(n):
        yy = jnp.where(n < 4, other_y, y)
        return ((z + offset_of(n % 4)) % 4) * 2 + yy

    def chunk_load(n):
        return pltpu.make_async_copy(
            hid.at[0, :, pl.ds(pl.multiple_of(chunk_q(n) * QROWS, 128), QROWS)],
            hch.at[n % 2],
            hs.at[n % 2],
        )

    gload = pltpu.make_async_copy(gra.at[0], G, ld.at[0])
    rest = [
        pltpu.make_async_copy(src, dst, ld.at[1 + n])
        for n, (src, dst) in enumerate(
            ((par_h.at[0], par), (mom_h.at[0], mom), (var_h.at[0], var), (anc_h, anc), (out_h, om))
        )
    ]
    chunk_load(0).start()
    gload.start()
    chunk_load(1).start()

    bar = pltpu.get_barrier_semaphore()
    peers = [xr, xl, zr, zl, ynb, (yh * 2 + 1 - co, f), ((1 - yh) * 2, f), ((1 - yh) * 2 + 1, f)]
    for peer in peers:
        pl.semaphore_signal(bar, inc=1, device_id=peer, device_id_type=MESH)

    def remote(src, dst, ss, rs, dev):
        return pltpu.make_async_remote_copy(
            src_ref=src, dst_ref=dst, send_sem=ss, recv_sem=rs, device_id=dev, device_id_type=MESH
        )

    parts = {True: (pl.ds(ROWS_Y, LATE // 2), pl.ds(ROWS_Y + LATE // 2, LATE // 2)), False: (pl.ds(0, HALF), pl.ds(HALF, HALF))}
    used = {True: pl.ds(0, LATE // 2), False: pl.ds(0, HALF)}

    def ring_send(k, p, s, d, kind, oth):
        tile = 0 if kind == 0 else 1 + d
        rows = parts[oth][1 - d if kind == 1 else d]
        return remote(
            ring.at[k, p, tile, rows], rA.at[k, s, d, kind, used[oth]], sA.at[k, p, d, kind], qA.at[k, s, d, kind], A[k][d]
        )

    def yearly(k, g, p):
        return remote(ey.at[k, p], rYE.at[k, g, p], sYE.at[k, p], qYE.at[k, g, p], ynb)

    def ysend(k, g, p):
        return remote(sy.at[k, p], rY.at[k, g, p], sY.at[k, p], qY.at[k, g, p], ynb)

    def csend(k, g, d, kind):
        rows = parts[False][1 - d if kind == 1 else d]
        src = c1.at[k, rows] if kind == 0 else tb.at[k, d, rows]
        return remote(src, rC.at[k, g, d, kind], sC.at[k, d, kind], qC.at[k, g, d, kind], C[k][d])

    def columns(k, g, b):
        return pl.ds(pl.multiple_of(1024 * k + 512 * b + 128 * g, 128), 128)

    def esend(k, g, b, slot, dev):
        return remote(st.at[k, b], rE.at[g, slot], sE.at[k, b], qE.at[g, slot], dev)

    def nsend(g, n, dev):
        cols = pl.ds(pl.multiple_of(512 * isl + 128 * g, 128), 128)
        return remote(nbuf.at[g], o_par.at[:, cols], sN.at[g, n], qN.at[isl, g], dev)

    def transpose_chunk(n):
        chunk_load(n).wait()
        base = chunk_q(n) * QROWS
        for j in range(QROWS // 128):
            rows = pl.ds(pl.multiple_of(base + 128 * j, 128), 128)
            hT[rows, :] = hch[n % 2, :, pl.ds(128 * j, 128)].T

        if isinstance(n, int):
            chunk_load(n + 2).start()
        else:

            @pl.when(n + 2 < 8)
            def _():
                chunk_load(n + 2).start()

    def by_y(p, body):
        @pl.when(p < 4)
        def _():
            body(True)

        @pl.when(p >= 4)
        def _():
            body(False)

    def stage0(k, t, before=None):
        g, p, s = t // 8, t % 8, t % SLOTS
        yy = jnp.where(p < 4, other_y, y)
        cc = (c_of[k] + offset_of(p % 4)) % 4

        @pl.when(g >= 1)
        def _():
            def free(oth):
                for d in range(2):
                    for kind in range(3):
                        ring_send(k, p, 0, d, kind, oth).wait_send()
                if oth:
                    yearly(k, g, p).wait_send()

            by_y(p, free)

        @pl.when(p >= 4)
        def _():
            yearly(k, g, p - 4).wait_recv()

        rhs = jnp.concatenate([G[:, columns(k, g, 0)], G[:, columns(k, g, 1)]], axis=1)
        for j, off in enumerate((2, 1, 3, 0)):
            if before is not None:
                before(j)
            r = block(k, (a_of[k] + off) % 4, yy, cc)
            lhs = hT[pl.ds(pl.multiple_of(r * ROWS, 32), ROWS), :]
            tile = jnp.dot(lhs, rhs, preferred_element_type=F32).astype(BF16)
            ring[k, p, j] = tile

            def finish(oth, j=j, tile=tile):
                if oth:
                    ey[k, p, j] = tile[:ROWS_Y]
                else:
                    ring[k, p, j, pl.ds(0, ROWS_Y)] = tile[:ROWS_Y] + rYE[k, g, p - 4, j]
                if j == 0:
                    for d in range(2):
                        ring_send(k, p, s, d, 0, oth).start()
                elif j < 3:
                    ring_send(k, p, s, j - 1, 1, oth).start()
                elif oth:
                    yearly(k, g, p).start()

            by_y(p, finish)

    def stage1(k, t):
        g, p, s = t // 8, t % 8, t % SLOTS

        def body(oth):
            for d in range(2):
                rows = parts[oth][d]
                ring_send(k, p, s, d, 0, oth).wait_recv()
                ring[k, p, 1 + d, rows] = ring[k, p, 1 + d, rows] + rA[k, s, d, 0, used[oth]]
                ring_send(k, p, s, d, 2, oth).start()

        by_y(p, body)

    def stage2(k, t):
        g, p, s = t // 8, t % 8, t % SLOTS

        def body(oth):
            for d in range(2):
                for kind in (1, 2):
                    ring_send(k, p, s, d, kind, oth).wait_recv()

            def total(q):
                return (
                    ring[k, p, 3, parts[oth][q]].astype(F32)
                    + rA[k, s, 0, 2 - q, used[oth]].astype(F32)
                    + rA[k, s, 1, 1 + q, used[oth]].astype(F32)
                )

            if oth:

                @pl.when(g >= 1)
                def _():
                    ysend(k, g, p).wait_send()

                for q in range(2):
                    sy[k, p, pl.ds(q * LATE // 2, LATE // 2)] = total(q).astype(BF16)
                ysend(k, g, p).start()
                return

            for q in range(2):
                tf[k, parts[False][q]] = total(q)
            ysend(k, g, p - 4).wait_recv()
            late = pl.ds(ROWS_Y, LATE)
            tf[k, late] = tf[k, late] + rY[k, g, p - 4].astype(F32)

            @pl.when(p == 4)
            def _():
                @pl.when(g >= 1)
                def _():
                    for d in range(2):
                        csend(k, g, d, 0).wait_send()

                c1[k] = tf[k].astype(BF16)
                for d in range(2):
                    csend(k, g, d, 0).start()

            for d in range(2):

                @pl.when(p == 5 + d)
                def _(d=d):
                    @pl.when(g >= 1)
                    def _():
                        for kind in (1, 2):
                            csend(k, g, d, kind).wait_send()

                    tb[k, d] = tf[k].astype(BF16)
                    csend(k, g, d, 1).start()

        by_y(p, body)

    def stage3(k, t):
        g, p = t // 8, t % 8
        for d in range(2):

            @pl.when(p == 5 + d)
            def _(d=d):
                rows = parts[False][d]
                csend(k, g, d, 0).wait_recv()
                tb[k, d, rows] = tb[k, d, rows] + rC[k, g, d, 0]
                csend(k, g, d, 2).start()

    corr_one = 1.0 - beta_one**INNER_STEP
    corr_two = 1.0 - beta_two**INNER_STEP

    def stage4(k, t):
        g, p = t // 8, t % 8

        @pl.when(p == 7)
        def _():
            @pl.when(g == 0)
            def _():
                if k == 0:
                    for copy in rest:
                        copy.wait()

            for d in range(2):
                for kind in (1, 2):
                    csend(k, g, d, kind).wait_recv()

            @pl.when(g >= 1)
            def _():
                @pl.when(yh == k)
                def _():
                    for b in range(2):

                        @pl.when(co != b)
                        def _(b=b):
                            esend(k, g, b, 0, (2 * k + b, f)).wait_send()

                @pl.when(yh != k)
                def _():
                    for b in range(2):
                        esend(k, g, b, 1 + co, (2 * k + b, f)).wait_send()

            for b in range(2):
                cols = columns(k, g, b)

                lanes = pl.ds(128 * b, 128)
                for q in range(2):
                    rows = parts[False][q]
                    grad = (
                        tf[k, rows, lanes]
                        + rC[k, g, 0, 2 - q, :, lanes].astype(F32)
                        + rC[k, g, 1, 1 + q, :, lanes].astype(F32)
                    )
                    here = par[rows, cols]
                    first = beta_one * mom[rows, cols] + (1.0 - beta_one) * grad
                    second = beta_two * var[rows, cols] + (1.0 - beta_two) * grad * grad
                    mom[rows, cols] = first
                    var[rows, cols] = second
                    update = first / corr_one / (jnp.sqrt(second / corr_two) + adam_eps)
                    stepped = here - inner_rate * (update + decay_rate * here)
                    st[k, b, rows] = stepped.astype(BF16)
                    par[rows, cols] = stepped

                @pl.when(jnp.logical_and(yh == k, co != b))
                def _(b=b):
                    esend(k, g, b, 0, (2 * k + b, f)).start()

                @pl.when(yh != k)
                def _(b=b):
                    esend(k, g, b, 1 + co, (2 * k + b, f)).start()

                pltpu.make_async_copy(mom.at[:, cols], o_first.at[0, :, cols], outs.at[0]).start()
                pltpu.make_async_copy(var.at[:, cols], o_second.at[0, :, cols], outs.at[1]).start()

    def others(k):
        return [(2 * k + 1 - co, f), (2 * (1 - k), f), (2 * (1 - k) + 1, f)]

    def stage5(k, t):
        g, p = t // 8, t % 8

        @pl.when(jnp.logical_and(p == 7, yh == k))
        def _():
            for slot in range(3):
                esend(k, g, 0, slot, (2 * k, f)).wait_recv()
            cols = pl.ds(pl.multiple_of(1024 * k + 512 * co + 128 * g, 128), 128)
            local = pl.ds(pl.multiple_of(128 * g, 128), 128)

            for rows in parts[False]:
                total = par[rows, cols]
                for slot in range(3):
                    total = total + rE[g, slot, rows].astype(F32)
                here = anc[rows, local]
                pseudo = here - total / 4.0
                moved = outer_beta * om[rows, local] + pseudo
                om[rows, local] = moved
                nbuf[g, rows] = (here - outer_rate * (pseudo + outer_beta * moved)).astype(BF16)
            for n, dev in enumerate(others(k)):
                nsend(g, n, dev).start()
            pltpu.make_async_copy(nbuf.at[g], o_par.at[:, cols], loc.at[g]).start()
            pltpu.make_async_copy(om.at[:, local], o_mom.at[:, local], outs.at[2]).start()

    def step(t, _):
        @pl.when(jnp.logical_and(t >= 1, t < 5))
        def _():
            transpose_chunk(t + 3)

        @pl.when(t == 8)
        def _():
            for copy in rest:
                copy.start()

        for delay, stage in ((0, stage0), (D1, stage1), (D2, stage2), (D3, stage3), (D4, stage4), (D5, stage5)):
            for k in range(2):
                tau = t - delay

                @pl.when(jnp.logical_and(tau >= 0, tau < STEPS))
                def _(tau=tau, k=k, stage=stage):
                    stage(k, tau)

        return 0

    transpose_chunk(0)
    gload.wait()
    pl.semaphore_wait(bar, len(peers))
    stage0(0, jnp.int32(0))

    def before(j):
        if j >= 1:
            transpose_chunk(j)

    stage0(1, jnp.int32(0), before)
    lax.fori_loop(1, STEPS + D5, step, 0)

    for k in range(2):
        for p in range(8):
            for d in range(2):
                for kind in range(3):
                    ring_send(k, p, 0, d, kind, p < 4).wait_send()
        for p in range(4):
            yearly(k, 0, p).wait_send()
            ysend(k, 0, p).wait_send()
        for d in range(2):
            for kind in range(3):
                csend(k, 0, d, kind).wait_send()
        for b in range(2):

            @pl.when(jnp.logical_or(yh != k, co != b))
            def _(k=k, b=b):
                esend(k, 0, b, 0, (2 * k + b, f)).wait_send()

    pltpu.make_async_copy(mom.at[:, pl.ds(0, D * GROUPS // 4)], o_first.at[0, :, pl.ds(0, D * GROUPS // 4)], outs.at[0]).wait()
    pltpu.make_async_copy(var.at[:, pl.ds(0, D * GROUPS // 4)], o_second.at[0, :, pl.ds(0, D * GROUPS // 4)], outs.at[1]).wait()
    pltpu.make_async_copy(om.at[:, pl.ds(0, 128 * GROUPS)], o_mom.at[:, pl.ds(0, 128 * GROUPS)], outs.at[2]).wait()
    for g in range(GROUPS):
        for k in range(2):

            @pl.when(yh == k)
            def _(k=k, g=g):
                for n, dev in enumerate(others(k)):
                    nsend(g, n, dev).wait_send()

        pltpu.make_async_copy(nbuf.at[g], o_par.at[:, pl.ds(0, 128)], loc.at[g]).wait()
        for i in range(4):

            @pl.when(isl != i)
            def _(i=i, g=g):
                cols = pl.ds(512 * i + 128 * g, 128)
                remote(nbuf.at[g], o_par.at[:, cols], sN.at[g, 0], qN.at[i, g], ynb).wait_recv()


PIECES = 2


def hand_on(*refs):
    sources, targets, held, sems = refs[:4], refs[4:8], refs[8:12], refs[12]
    rows = ROWS // PIECES
    pairs = []
    for n, (src, dst, mid) in enumerate(zip(sources, targets, held)):
        for m in range(PIECES):
            part = (slice(None),) * (len(src.shape) - 2) + (pl.ds(m * rows, rows),)
            pairs.append(
                (
                    pltpu.make_async_copy(src.at[part], mid.at[part], sems.at[0, n, m]),
                    pltpu.make_async_copy(mid.at[part], dst.at[part], sems.at[1, n, m]),
                )
            )
    for load, _ in pairs:
        load.start()
    for load, store in pairs:
        load.wait()
        store.start()
    for _, store in pairs:
        store.wait()


def on_device(hidden, grad_out, inner_params, first_moment, second_moment, anchor, outer_momentum):
    dma = pltpu.SemaphoreType.DMA
    vm = pltpu.VMEM
    tile, half, narrow = (ROWS, WIDE), (HALF, WIDE), (ROWS, 128)
    any_spec = pl.BlockSpec(memory_space=pl.ANY)
    shapes = (
        jax.ShapeDtypeStruct((ROWS, D), BF16),
        jax.ShapeDtypeStruct((ROWS, 512), F32),
        jax.ShapeDtypeStruct((1, ROWS, D), F32),
        jax.ShapeDtypeStruct((1, ROWS, D), F32),
    )
    results = pl.pallas_call(
        kernel,
        name="window",
        out_shape=shapes,
        in_specs=[any_spec] * 7,
        out_specs=(any_spec,) * 4,
        scratch_shapes=[
            vm((2, TOK, QROWS), BF16),
            vm((FF, TOK), BF16),
            vm((TOK, D), BF16),
            vm((ROWS, D), F32),
            vm((ROWS, D), F32),
            vm((ROWS, D), F32),
            vm((ROWS, 512), F32),
            vm((ROWS, 512), F32),
            vm((2, 8, 4) + tile, BF16),
            vm((2, 4, 4, ROWS_Y, WIDE), BF16),
            vm((2, 4, LATE, WIDE), BF16),
            vm((2,) + tile, BF16),
            vm((2, 2) + tile, BF16),
            vm((2,) + tile, F32),
            vm((2, 2) + narrow, BF16),
            vm((GROUPS,) + narrow, BF16),
            vm((2, SLOTS, 2, 3) + half, BF16),
            vm((2, GROUPS, 4, 4, ROWS_Y, WIDE), BF16),
            vm((2, GROUPS, 4, LATE, WIDE), BF16),
            vm((2, GROUPS, 2, 3) + half, BF16),
            vm((GROUPS, 3) + narrow, BF16),
            dma((6,)),
            dma((2,)),
            dma((2, 8, 2, 3)),
            dma((2, 4)),
            dma((2, 4)),
            dma((2, 2, 3)),
            dma((2, 2)),
            dma((GROUPS, 3)),
            dma((3,)),
            dma((GROUPS,)),
            dma((2, SLOTS, 2, 3)),
            dma((2, GROUPS, 4)),
            dma((2, GROUPS, 4)),
            dma((2, GROUPS, 2, 3)),
            dma((GROUPS, 3)),
            dma((4, GROUPS)),
        ],
        compiler_params=pltpu.CompilerParams(
            collective_id=0, has_side_effects=True, vmem_limit_bytes=60 * 1024 * 1024
        ),
        cost_estimate=pl.CostEstimate(flops=2 * TOK * FF * D, bytes_accessed=32 << 20, transcendentals=0),
    )(hidden, grad_out, inner_params, first_moment, second_moment, anchor, outer_momentum)
    return pl.pallas_call(
        hand_on,
        name="hand_on",
        out_shape=shapes,
        in_specs=[any_spec] * 4,
        out_specs=(any_spec,) * 4,
        scratch_shapes=[vm(shape.shape, shape.dtype) for shape in shapes] + [dma((2, 4, PIECES))],
    )(*results)


def solution(mesh):
    placed = (
        P("island", "fsdp", None),
        P("island", "fsdp", None),
        P("island", "fsdp", None),
        P("island", "fsdp", None),
        P("island", "fsdp", None),
        P("fsdp", "island"),
        P("fsdp", "island"),
    )
    return jax.shard_map(
        on_device,
        mesh=mesh,
        in_specs=placed,
        out_specs=(
            P("fsdp", None),
            P("fsdp", "island"),
            P("island", "fsdp", None),
            P("island", "fsdp", None),
        ),
        check_vma=False,
    )
```

```python
import functools

import jax
import jax.numpy as jnp
from jax import lax
from jax.experimental import pallas as pl
from jax.experimental.pallas import tpu as pltpu
from jax.sharding import PartitionSpec as P

INNER_STEP = 20
beta_one = 0.9
beta_two = 0.95
inner_rate = 0.01
decay_rate = 0.1
adam_eps = 1e-08
outer_rate = 0.7
outer_beta = 0.9

MESH = pl.DeviceIdType.MESH
TOK, FF, D = 768, 7168, 2048
ROWS, HALF = 224, 112
QROWS = 4 * ROWS
WIDE = 256
GROUPS = 4
STEPS = 8 * GROUPS
SLOTS = 16
D1, D2, D3, D4, D5, D6, D7 = 2, 4, 6, 8, 9, 12, 15
F32, BF16 = jnp.float32, jnp.bfloat16


EARLY = (32, 32)


def offset_of(q):
    return jnp.where(q == 2, 3, jnp.where(q == 3, 0, 2 - q))


def kernel(
    hid, gra, par_h, mom_h, var_h, anc_h, out_h,
    o_par, om, mom, var,
    hch, hT, G, par, anc,
    ring, ey, sy, c1, tb, tf, st, ps, nbuf,
    rA, rYE, rY, rC, rE,
    ld, hs, sA, sYE, sY, sC, sE, sP, sN, sR,
    qA, qYE, qY, qC, qE, qN,
):
    isl, f = lax.axis_index("island"), lax.axis_index("fsdp")
    yh, co = isl // 2, isl % 2
    z, y, x = f // 8, (f // 4) % 2, f % 4
    other_y = 1 - y

    def fs(zz, yy, xx):
        return zz * 8 + yy * 4 + xx

    xr, xl = (isl, fs(z, y, (x + 1) % 4)), (isl, fs(z, y, (x + 3) % 4))
    zr, zl = (isl, fs((z + 1) % 4, y, x)), (isl, fs((z + 3) % 4, y, x))
    ynb = (isl, fs(z, other_y, x))
    A = ((xr, xl), (zr, zl))
    C = ((zr, zl), (xr, xl))
    a_of = (x, z)
    c_of = (z, x)

    def block(k, a, yy, c):
        return fs(c, yy, a) if k == 0 else fs(a, yy, c)

    def chunk_q(n):
        yy = jnp.where(n < 4, other_y, y)
        return ((z + offset_of(n % 4)) % 4) * 2 + yy

    def chunk_load(n):
        return pltpu.make_async_copy(
            hid.at[0, :, pl.ds(pl.multiple_of(chunk_q(n) * QROWS, 128), QROWS)],
            hch.at[n % 2],
            hs.at[n % 2],
        )

    gload = pltpu.make_async_copy(gra.at[0], G, ld.at[0])
    rest = [
        pltpu.make_async_copy(src, dst, ld.at[1 + n])
        for n, (src, dst) in enumerate(
            ((par_h.at[0], par), (mom_h.at[0], mom), (var_h.at[0], var), (anc_h, anc), (out_h, om))
        )
    ]
    chunk_load(0).start()
    gload.start()
    chunk_load(1).start()

    bar = pltpu.get_barrier_semaphore()
    partner, far = (yh * 2 + 1 - co, f), ((1 - yh) * 2 + co, f)
    peers = [xr, xl, zr, zl, ynb, partner, far]
    for peer in peers:
        pl.semaphore_signal(bar, inc=1, device_id=peer, device_id_type=MESH)

    def remote(src, dst, ss, rs, dev):
        return pltpu.make_async_remote_copy(
            src_ref=src, dst_ref=dst, send_sem=ss, recv_sem=rs, device_id=dev, device_id_type=MESH
        )

    def parts(piece):
        oth, early = piece
        if not oth:
            return ((0, HALF), (HALF, HALF))
        size = -(-(ROWS - early) // 32) * 16
        return ((early, size), (early + size, ROWS - early - size))

    def ring_send(k, p, s, d, kind, piece):
        tile = 0 if kind == 0 else 1 + d
        start, size = parts(piece)[1 - d if kind == 1 else d]
        return remote(
            ring.at[k, p, tile, pl.ds(start, size)],
            rA.at[k, s, d, kind, pl.ds(0, size)],
            sA.at[k, p, d, kind],
            qA.at[k, s, d, kind],
            A[k][d],
        )

    def yearly(k, g, p, early):
        rows = pl.ds(0, early)
        return remote(ey.at[k, p, :, rows], rYE.at[k, g, p, :, rows], sYE.at[k, p], qYE.at[k, g, p], ynb)

    def ysend(k, g, p, early):
        rows = pl.ds(0, ROWS - early)
        return remote(sy.at[k, p, rows], rY.at[k, g, p, rows], sY.at[k, p], qY.at[k, g, p], ynb)

    halves = (pl.ds(0, HALF), pl.ds(HALF, HALF))

    def csend(k, g, d, kind):
        rows = halves[1 - d if kind == 1 else d]
        src = c1.at[k, rows] if kind == 0 else tb.at[k, d, rows]
        return remote(src, rC.at[k, g, d, kind], sC.at[k, d, kind], qC.at[k, g, d, kind], C[k][d])

    def columns(k, g, b):
        return pl.ds(pl.multiple_of(1024 * k + 512 * b + 128 * g, 128), 128)

    def esend(k, g):
        return remote(st.at[k, 1 - co], rE.at[k, g, 0], sE.at[k], qE.at[k, g, 0], partner)

    def psend(k, g):
        return remote(ps, rE.at[k, g, 1], sP, qE.at[k, g, 1], far)

    def param_columns(island, g):
        return pl.ds(pl.multiple_of(512 * island + 128 * g, 128), 128)

    def nsend(g, n):
        return remote(nbuf.at[g], o_par.at[:, param_columns(isl, g)], sN.at[g, n], qN.at[isl, g], (partner, far)[n])

    def relay(g):
        owner = 2 * (1 - yh) + co
        here = o_par.at[:, param_columns(owner, g)]
        return remote(here, here, sR.at[g], qN.at[owner, g], partner)

    def transpose_chunk(n):
        chunk_load(n).wait()
        base = chunk_q(n) * QROWS
        for j in range(QROWS // 128):
            rows = pl.ds(pl.multiple_of(base + 128 * j, 128), 128)
            hT[rows, :] = hch[n % 2, :, pl.ds(128 * j, 128)].T

        if isinstance(n, int):
            chunk_load(n + 2).start()
        else:

            @pl.when(n + 2 < 8)
            def _():
                chunk_load(n + 2).start()

    def by_piece(p, body):
        for n, piece in enumerate(((True, EARLY[0]), (True, EARLY[1]), (False, EARLY[0]), (False, EARLY[1]))):

            @pl.when(p // 2 == n)
            def _(piece=piece):
                body(piece)

    def stage0(k, t, before=None):
        g, p, s = t // 8, t % 8, t % SLOTS
        yy = jnp.where(p < 4, other_y, y)
        cc = (c_of[k] + offset_of(p % 4)) % 4

        @pl.when(g >= 1)
        def _():
            def free(piece):
                for d in range(2):
                    for kind in range(3):
                        ring_send(k, p, 0, d, kind, piece).wait_send()
                if piece[0]:
                    yearly(k, g, p, piece[1]).wait_send()

            by_piece(p, free)

        def arrived(piece):
            if not piece[0]:
                yearly(k, g, p - 4, piece[1]).wait_recv()

        by_piece(p, arrived)

        rhs = jnp.concatenate([G[:, columns(k, g, 0)], G[:, columns(k, g, 1)]], axis=1)
        for j, off in enumerate((2, 1, 3, 0)):
            if before is not None:
                before(j)
            r = block(k, (a_of[k] + off) % 4, yy, cc)
            lhs = hT[pl.ds(pl.multiple_of(r * ROWS, 32), ROWS), :]
            tile = jnp.dot(lhs, rhs, preferred_element_type=F32).astype(BF16)
            ring[k, p, j] = tile

            def finish(piece, j=j, tile=tile):
                oth, early = piece
                if oth:
                    ey[k, p, j, pl.ds(0, early)] = tile[:early]
                else:
                    ring[k, p, j, pl.ds(0, early)] = tile[:early] + rYE[k, g, p - 4, j, pl.ds(0, early)]
                if j == 0:
                    for d in range(2):
                        ring_send(k, p, s, d, 0, piece).start()
                elif j < 3:
                    ring_send(k, p, s, j - 1, 1, piece).start()
                elif oth:
                    yearly(k, g, p, early).start()

            by_piece(p, finish)

    def stage1(k, t):
        g, p, s = t // 8, t % 8, t % SLOTS

        def body(piece):
            for d in range(2):
                start, size = parts(piece)[d]
                rows = pl.ds(start, size)
                ring_send(k, p, s, d, 0, piece).wait_recv()
                ring[k, p, 1 + d, rows] = ring[k, p, 1 + d, rows] + rA[k, s, d, 0, pl.ds(0, size)]
                ring_send(k, p, s, d, 2, piece).start()

        by_piece(p, body)

    def stage2(k, t):
        g, p, s = t // 8, t % 8, t % SLOTS

        def body(piece):
            oth, early = piece
            for d in range(2):
                for kind in (1, 2):
                    ring_send(k, p, s, d, kind, piece).wait_recv()

            def total(q):
                start, size = parts(piece)[q]
                return (
                    ring[k, p, 3, pl.ds(start, size)].astype(F32)
                    + rA[k, s, 0, 2 - q, pl.ds(0, size)].astype(F32)
                    + rA[k, s, 1, 1 + q, pl.ds(0, size)].astype(F32)
                )

            if oth:

                @pl.when(g >= 1)
                def _():
                    ysend(k, g, p, early).wait_send()

                for q in range(2):
                    start, size = parts(piece)[q]
                    sy[k, p, pl.ds(start - early, size)] = total(q).astype(BF16)
                ysend(k, g, p, early).start()
                return

            for q in range(2):
                tf[k, halves[q]] = total(q)
            ysend(k, g, p - 4, early).wait_recv()
            late = pl.ds(early, ROWS - early)
            tf[k, late] = tf[k, late] + rY[k, g, p - 4, pl.ds(0, ROWS - early)].astype(F32)

            @pl.when(p == 4)
            def _():
                @pl.when(g >= 1)
                def _():
                    for d in range(2):
                        csend(k, g, d, 0).wait_send()

                c1[k] = tf[k].astype(BF16)
                for d in range(2):
                    csend(k, g, d, 0).start()

            for d in range(2):

                @pl.when(p == 5 + d)
                def _(d=d):
                    @pl.when(g >= 1)
                    def _():
                        for kind in (1, 2):
                            csend(k, g, d, kind).wait_send()

                    tb[k, d] = tf[k].astype(BF16)
                    csend(k, g, d, 1).start()

        by_piece(p, body)

    def stage3(k, t):
        g, p = t // 8, t % 8
        for d in range(2):

            @pl.when(p == 5 + d)
            def _(d=d):
                rows = halves[d]
                csend(k, g, d, 0).wait_recv()
                tb[k, d, rows] = tb[k, d, rows] + rC[k, g, d, 0]
                csend(k, g, d, 2).start()

    corr_one = 1.0 - beta_one**INNER_STEP
    corr_two = 1.0 - beta_two**INNER_STEP

    def stage4(k, t):
        g, p = t // 8, t % 8

        @pl.when(p == 7)
        def _():
            @pl.when(g == 0)
            def _():
                if k == 0:
                    for copy in rest:
                        copy.wait()

            for d in range(2):
                for kind in (1, 2):
                    csend(k, g, d, kind).wait_recv()

            @pl.when(g >= 1)
            def _():
                esend(k, g).wait_send()

            for b in (1 - co, co):
                cols = columns(k, g, b)
                lanes = pl.ds(pl.multiple_of(128 * b, 128), 128)
                for q in range(2):
                    rows = halves[q]
                    grad = (
                        tf[k, rows, lanes]
                        + rC[k, g, 0, 2 - q, :, lanes].astype(F32)
                        + rC[k, g, 1, 1 + q, :, lanes].astype(F32)
                    )
                    here = par[rows, cols]
                    first = beta_one * mom[rows, cols] + (1.0 - beta_one) * grad
                    second = beta_two * var[rows, cols] + (1.0 - beta_two) * grad * grad
                    mom[rows, cols] = first
                    var[rows, cols] = second
                    update = first / corr_one / (jnp.sqrt(second / corr_two) + adam_eps)
                    stepped = here - inner_rate * (update + decay_rate * here)
                    st[k, b, rows] = stepped.astype(BF16)
                    par[rows, cols] = stepped

                if b is not co:
                    esend(k, g).start()

    def stage5(k, t):
        g, p = t // 8, t % 8

        @pl.when(p == 7)
        def _():
            esend(k, g).wait_recv()

            @pl.when(yh != k)
            def _():
                @pl.when(g >= 1)
                def _():
                    psend(k, g).wait_send()

                for rows in halves:
                    ps[rows] = (par[rows, columns(k, g, co)] + rE[k, g, 0, rows].astype(F32)).astype(BF16)
                psend(k, g).start()

    def stage6(k, t):
        g, p = t // 8, t % 8

        @pl.when(jnp.logical_and(p == 7, yh == k))
        def _():
            psend(k, g).wait_recv()
            local = pl.ds(pl.multiple_of(128 * g, 128), 128)
            for rows in halves:
                total = par[rows, columns(k, g, co)] + rE[k, g, 0, rows].astype(F32) + rE[k, g, 1, rows].astype(F32)
                here = anc[rows, local]
                pseudo = here - total / 4.0
                moved = outer_beta * om[rows, local] + pseudo
                om[rows, local] = moved
                nbuf[g, rows] = (here - outer_rate * (pseudo + outer_beta * moved)).astype(BF16)
            for n in (1, 0):
                nsend(g, n).start()
            o_par[:, param_columns(isl, g)] = nbuf[g]

    def stage7(k, t):
        g, p = t // 8, t % 8

        @pl.when(jnp.logical_and(p == 7, yh != k))
        def _():
            relay(g).wait_recv()
            relay(g).start()

    def step(t, _):
        @pl.when(jnp.logical_and(t >= 1, t < 5))
        def _():
            transpose_chunk(t + 3)

        @pl.when(t == 8)
        def _():
            for copy in rest:
                copy.start()

        for delay, stage in ((0, stage0), (D1, stage1), (D2, stage2), (D3, stage3), (D4, stage4), (D5, stage5), (D6, stage6), (D7, stage7)):
            for k in range(2):
                tau = t - delay

                @pl.when(jnp.logical_and(tau >= 0, tau < STEPS))
                def _(tau=tau, k=k, stage=stage):
                    stage(k, tau)

        return 0

    transpose_chunk(0)
    gload.wait()
    pl.semaphore_wait(bar, len(peers))
    stage0(0, jnp.int32(0))

    def before(j):
        if j >= 1:
            transpose_chunk(j)

    stage0(1, jnp.int32(0), before)
    lax.fori_loop(1, STEPS + D7, step, 0)

    for k in range(2):
        for p in range(8):
            for d in range(2):
                for kind in range(3):
                    ring_send(k, p, 0, d, kind, (p < 4, EARLY[p % 4 // 2])).wait_send()
        for p in range(4):
            yearly(k, 0, p, EARLY[p // 2]).wait_send()
            ysend(k, 0, p, EARLY[p // 2]).wait_send()
        for d in range(2):
            for kind in range(3):
                csend(k, 0, d, kind).wait_send()
        esend(k, 0).wait_send()
    psend(0, 0).wait_send()
    for g in range(GROUPS):
        for n in range(2):
            nsend(g, n).wait_send()
        relay(g).wait_send()
        for owner in (2 * yh + 1 - co, 2 * (1 - yh) + 1 - co):
            remote(nbuf.at[g], o_par.at[:, param_columns(owner, g)], sN.at[g, 0], qN.at[owner, g], partner).wait_recv()


PIECES = 2


def hand_on(*refs):
    sources, targets, sems = refs[:4], refs[4:8], refs[8]
    copies = []
    for n, (src, dst) in enumerate(zip(sources, targets)):
        for m in range(PIECES):
            rows = pl.ds(m * (ROWS // PIECES), ROWS // PIECES)
            to = dst.at[0, rows] if len(dst.shape) == 3 else dst.at[rows]
            copies.append(pltpu.make_async_copy(src.at[rows], to, sems.at[n, m]))
    for copy in copies:
        copy.start()
    for copy in copies:
        copy.wait()


def on_device(hidden, grad_out, inner_params, first_moment, second_moment, anchor, outer_momentum):
    dma = pltpu.SemaphoreType.DMA
    vm = pltpu.VMEM
    tile, half, narrow = (ROWS, WIDE), (HALF, WIDE), (ROWS, 128)
    any_spec = pl.BlockSpec(memory_space=pl.ANY)
    shapes = (
        jax.ShapeDtypeStruct((ROWS, D), BF16),
        jax.ShapeDtypeStruct((ROWS, 512), F32),
        jax.ShapeDtypeStruct((1, ROWS, D), F32),
        jax.ShapeDtypeStruct((1, ROWS, D), F32),
    )
    results = pl.pallas_call(
        kernel,
        name="window",
        out_shape=tuple(vm(shape.shape[-2:], shape.dtype) for shape in shapes),
        in_specs=[any_spec] * 7,
        out_specs=(pl.BlockSpec(memory_space=pltpu.VMEM),) * 4,
        scratch_shapes=[
            vm((2, TOK, QROWS), BF16),
            vm((FF, TOK), BF16),
            vm((TOK, D), BF16),
            vm((ROWS, D), F32),
            vm((ROWS, 512), F32),
            vm((2, 8, 4) + tile, BF16),
            vm((2, 4, 4, max(EARLY), WIDE), BF16),
            vm((2, 4, ROWS - min(EARLY), WIDE), BF16),
            vm((2,) + tile, BF16),
            vm((2, 2) + tile, BF16),
            vm((2,) + tile, F32),
            vm((2, 2) + narrow, BF16),
            vm(narrow, BF16),
            vm((GROUPS,) + narrow, BF16),
            vm((2, SLOTS, 2, 3) + half, BF16),
            vm((2, GROUPS, 4, 4, max(EARLY), WIDE), BF16),
            vm((2, GROUPS, 4, ROWS - min(EARLY), WIDE), BF16),
            vm((2, GROUPS, 2, 3) + half, BF16),
            vm((2, GROUPS, 2) + narrow, BF16),
            dma((6,)),
            dma((2,)),
            dma((2, 8, 2, 3)),
            dma((2, 4)),
            dma((2, 4)),
            dma((2, 2, 3)),
            dma((2,)),
            dma,
            dma((GROUPS, 2)),
            dma((GROUPS,)),
            dma((2, SLOTS, 2, 3)),
            dma((2, GROUPS, 4)),
            dma((2, GROUPS, 4)),
            dma((2, GROUPS, 2, 3)),
            dma((2, GROUPS, 2)),
            dma((4, GROUPS)),
        ],
        compiler_params=pltpu.CompilerParams(
            collective_id=0, has_side_effects=True, vmem_limit_bytes=54 * 1024 * 1024
        ),
        cost_estimate=pl.CostEstimate(flops=2 * TOK * FF * D, bytes_accessed=32 << 20, transcendentals=0),
    )(hidden, grad_out, inner_params, first_moment, second_moment, anchor, outer_momentum)
    return pl.pallas_call(
        hand_on,
        name="hand_on",
        out_shape=shapes,
        in_specs=[pl.BlockSpec(memory_space=pltpu.VMEM)] * 4,
        out_specs=(any_spec,) * 4,
        scratch_shapes=[dma((4, PIECES))],
        compiler_params=pltpu.CompilerParams(vmem_limit_bytes=1024 * 1024),
    )(*(pltpu.with_memory_space_constraint(result, pltpu.VMEM) for result in results))


def solution(mesh):
    placed = (
        P("island", "fsdp", None),
        P("island", "fsdp", None),
        P("island", "fsdp", None),
        P("island", "fsdp", None),
        P("island", "fsdp", None),
        P("fsdp", "island"),
        P("fsdp", "island"),
    )
    return jax.shard_map(
        on_device,
        mesh=mesh,
        in_specs=placed,
        out_specs=(
            P("fsdp", None),
            P("fsdp", "island"),
            P("island", "fsdp", None),
            P("island", "fsdp", None),
        ),
        check_vma=False,
    )
```
